32 devices in a mesh: sec: 4 (over x, core), op: 8 (over z, y).
Axes of the slice: x: 2, y: 2, z: 4, core: 2. Of those that a mesh axis runs over, the one named last changes fastest.
Arguments:
- psi_blocks: bfloat16 [1536, 384], P('sec'), may hold values from -0.078125 to 0.078125
- sector_rows: int32 [4], P('sec'), may hold values from 96 to 384, as said below
- kept_cols: int32 [4], P('sec'), may hold values from 96 to 384, as said below
- basis: bfloat16 [1536, 384], P('sec'), may hold values from -0.3125 to 0.3125
- left_ops: bfloat16 [16, 1536, 1152], P('op', 'sec'), may hold values from -6 to 6
- right_ops: bfloat16 [16, 4, 3, 384, 384], P('op', 'sec'), may hold values from -0.1875 to 0.1875
Outputs:
- sigma: bfloat16 [1536, 384], P(('sec', 'op'))
- renorm_ops: bfloat16 [16, 1536, 1152], P(None, ('sec', 'op'))
The draws below stay inside these ranges and needn't reach their ends.
Inputs may be any that keep to these rules, and one draw needn't show every extreme that they name: `sector_rows`: some sector has exactly 384 live states and another exactly 96. `kept_cols`: some sector keeps exactly 384 states and another exactly 96.
All inputs are finite; a program needn't handle non-finite values.
Results may differ from the reference program's by a relative error of at most 0.0049.
Values may be sent and summed in bfloat16 or wider, within the bound.
A program may use at most 64 MiB of HBM per device.

```python
import jax
import jax.numpy as jnp
from jax import lax

ROWS_DEV = 384
NR = 384
KP = 384
OPS = 16
SECTORS = 4
BOND = 1536
KEPT = 1536


def bounded_counts(key, most):
    first_key, second_key, third_key = jax.random.split(key, 3)
    counts = jax.random.randint(first_key, (SECTORS,), most // 4, most + 1)
    highest = jax.random.randint(second_key, (), 0, SECTORS)
    lowest = (highest + 1 + jax.random.randint(third_key, (), 0, SECTORS - 1)) % SECTORS
    counts = counts.at[highest].set(most)
    counts = counts.at[lowest].set(most // 4)
    return counts.astype(jnp.int32)


def draw_sector_rows(key, part):
    key = jax.random.fold_in(key, 11)
    return bounded_counts(key, ROWS_DEV)


def draw_kept_cols(key, part):
    key = jax.random.fold_in(key, 23)
    return bounded_counts(key, KP)


def level_of(rng, dims, cuts, low, largest):
    level = 1.0
    for axis_at, parts in cuts:
        draws = jax.random.uniform(jax.random.fold_in(jax.random.fold_in(rng, 6), axis_at), (parts,), jnp.float32, low / len(cuts), largest / len(cuts))
        level = level * jnp.repeat(jnp.exp(draws), dims[axis_at] // parts).reshape((-1,) + (1,) * (len(dims) - 1 - axis_at))
    return level


def scatter_about(stream_key, dims, deviation, bound, cuts=(), held_as=jnp.bfloat16):
    values = deviation * jax.random.normal(stream_key, dims, jnp.float32)
    if cuts:
        values = values * level_of(stream_key, dims, cuts, -0.22, 0.18)
    return jnp.clip(values, -bound, bound).astype(held_as)


def setup_inputs(seed: int = 0) -> dict:
    keys = jax.random.split(jax.random.key(seed), 7)
    psi_blocks = scatter_about(keys[0], (BOND, NR), (ROWS_DEV * OPS) ** -0.5, 0.078125, ((0, 4),))
    sector_rows = draw_sector_rows(jax.random.fold_in(keys[6], 71), 0)
    kept_cols = draw_kept_cols(jax.random.fold_in(keys[6], 71), 0)
    basis = scatter_about(keys[3], (BOND, KP), ROWS_DEV ** -0.5, 0.3125, ((0, 4),))
    left_ops = scatter_about(keys[4], (OPS, BOND, 3 * ROWS_DEV), 1.0, 6.0, ((0, 8), (1, 4)))
    right_ops = scatter_about(keys[5], (OPS, SECTORS, 3, NR, NR), (3 * NR) ** -0.5, 0.1875, ((0, 8), (1, 4)))
    return dict(psi_blocks=psi_blocks, sector_rows=sector_rows, kept_cols=kept_cols, basis=basis, left_ops=left_ops, right_ops=right_ops)


def reference(psi_blocks, sector_rows, kept_cols, basis, left_ops, right_ops):
    place = jnp.arange(ROWS_DEV, dtype=jnp.int32)
    live_mask = place[None, :] < sector_rows[:, None]
    column_mask = jnp.arange(KP, dtype=jnp.int32)[None, :] < kept_cols[:, None]
    psi_live = jnp.where(live_mask[:, :, None], psi_blocks.reshape(SECTORS, ROWS_DEV, NR), jnp.zeros((), jnp.bfloat16)).reshape(BOND, NR)
    both_mask = live_mask[:, :, None] & column_mask[:, None, :]
    basis_live = jnp.where(both_mask, basis.reshape(SECTORS, ROWS_DEV, KP), jnp.zeros((), jnp.bfloat16)).reshape(BOND, KP)
    psi_padded = jnp.concatenate([jnp.zeros((ROWS_DEV, NR), jnp.bfloat16), psi_live, jnp.zeros((ROWS_DEV, NR), jnp.bfloat16)], axis=0)
    basis_padded = jnp.concatenate([jnp.zeros((ROWS_DEV, KP), jnp.bfloat16), basis_live, jnp.zeros((ROWS_DEV, KP), jnp.bfloat16)], axis=0)

    def one_sector(sector):
        first = (sector * ROWS_DEV).astype(jnp.int32)
        near_state = lax.dynamic_slice_in_dim(psi_padded, first, 3 * ROWS_DEV, 0)
        near_basis = lax.dynamic_slice_in_dim(basis_padded, first, 3 * ROWS_DEV, 0)
        own_basis = lax.dynamic_slice_in_dim(basis_live, first, ROWS_DEV, 0).astype(jnp.float32)
        lefts = lax.dynamic_slice_in_dim(left_ops, first, ROWS_DEV, 1)
        rights = lax.dynamic_index_in_dim(right_ops, sector, 1, keepdims=False)
        accumulated = jnp.zeros((ROWS_DEV, NR), jnp.float32)
        pieces = []
        for neighbor in range(3):
            left_part = lefts[:, :, neighbor * ROWS_DEV:(neighbor + 1) * ROWS_DEV].astype(jnp.float32)
            near_part = near_state[neighbor * ROWS_DEV:(neighbor + 1) * ROWS_DEV].astype(jnp.float32)
            product = jnp.einsum('krs,sn->krn', left_part, near_part).astype(jnp.bfloat16)
            product = lax.optimization_barrier(product).astype(jnp.float32)
            accumulated = accumulated + jnp.einsum('krn,kmn->rm', product, rights[:, neighbor].astype(jnp.float32))
            basis_part = near_basis[neighbor * ROWS_DEV:(neighbor + 1) * ROWS_DEV].astype(jnp.float32)
            vmatrix = jnp.einsum('krs,sc->krc', left_part, basis_part).astype(jnp.bfloat16)
            vmatrix = lax.optimization_barrier(vmatrix).astype(jnp.float32)
            pieces.append(jnp.einsum('rc,krq->kcq', own_basis, vmatrix).astype(jnp.bfloat16))
        alive = place < sector_rows[sector]
        accumulated = jnp.where(alive[:, None], accumulated, jnp.float32(0.0)).astype(jnp.bfloat16)
        return accumulated, jnp.concatenate(pieces, axis=2)

    sigma_blocks, renorm_blocks = lax.map(one_sector, jnp.arange(SECTORS, dtype=jnp.int32))
    sigma = sigma_blocks.reshape(BOND, NR)
    renorm_ops = jnp.transpose(renorm_blocks, (1, 0, 2, 3)).reshape(OPS, KEPT, 3 * KP)
    return sigma, renorm_ops
```

```python
import functools

import jax
import jax.numpy as jnp
from jax import lax
from jax.experimental import pallas as pl
from jax.experimental.pallas import tpu as pltpu
from jax.sharding import PartitionSpec as P

MESH = pl.DeviceIdType.MESH


def kernel(
    sec_n, op_n, rows_ref, cols_ref, psi_hbm, basis_hbm, left_hbm, right_hbm,
    sigma_ref, renorm_ref,
    psi_raw, basis_raw, near_psi, near_basis, basis_t, left, right, full, stage,
    total, sigma_stage, sigma_parts,
    load_sem, halo_send, halo_recv, send_sem, recv_sem, sigma_send, sigma_recv,
):
    ops, row_count, _ = left.shape
    kept = basis_raw.shape[1]
    width = psi_raw.shape[1]
    share = stage.shape[2]
    sigma_share = sigma_stage.shape[1]
    sec = lax.axis_index("sec")
    op = lax.axis_index("op")
    has = (sec > 0, None, sec < sec_n - 1)

    loads = [pltpu.make_async_copy(basis_hbm, basis_raw, load_sem.at[0])]
    loads += [pltpu.make_async_copy(left_hbm.at[k], left.at[k], load_sem.at[1 + k]) for k in range(ops)]
    loads += [
        pltpu.make_async_copy(psi_hbm, psi_raw, load_sem.at[1 + ops]),
        pltpu.make_async_copy(right_hbm, right, load_sem.at[2 + ops]),
    ]
    for load in loads:
        load.start()

    barrier = pltpu.get_barrier_semaphore()

    def greet(step, carry):
        pl.semaphore_signal(
            barrier, inc=1, device_id=(sec, lax.rem(op + step, op_n)), device_id_type=MESH
        )
        return carry

    for d in (0, 2):
        @pl.when(has[d])
        def _():
            pl.semaphore_signal(barrier, inc=1, device_id=(sec + d - 1, op), device_id_type=MESH)
    lax.fori_loop(1, op_n, greet, 0)

    live = lax.broadcasted_iota(jnp.int32, (row_count, kept), 0) < rows_ref[0]
    live_kept = live & (lax.broadcasted_iota(jnp.int32, (row_count, kept), 1) < cols_ref[0])
    loads[0].wait()
    masked = jnp.where(live_kept, basis_raw[...].astype(jnp.float32), 0.0)
    near_basis[1] = masked.astype(jnp.bfloat16)
    live_state = lax.broadcasted_iota(jnp.int32, (row_count, width), 0) < rows_ref[0]
    loads[1 + ops].wait()
    near_psi[1] = jnp.where(live_state, psi_raw[...].astype(jnp.float32), 0.0).astype(jnp.bfloat16)

    beside = (sec > 0).astype(jnp.int32) + (sec < sec_n - 1).astype(jnp.int32)
    pl.semaphore_wait(barrier, op_n - 1 + beside)

    def halo(near, at, d):
        return pltpu.make_async_remote_copy(
            src_ref=near.at[1], dst_ref=near.at[2 - d],
            send_sem=halo_send.at[at, d], recv_sem=halo_recv.at[at, 2 - d],
            device_id=(sec + d - 1, op), device_id_type=MESH,
        )

    def arrival(near, at, d):
        return pltpu.make_async_remote_copy(
            src_ref=near.at[1], dst_ref=near.at[d],
            send_sem=halo_send.at[at, d], recv_sem=halo_recv.at[at, d],
            device_id=(sec + d - 1, op), device_id_type=MESH,
        )

    for at, near in ((0, near_basis), (1, near_psi)):
        for d in (0, 2):
            @pl.when(has[d])
            def _():
                halo(near, at, d).start()

    basis_t[...] = masked.T.astype(jnp.bfloat16)

    def piece(k, d, source, slot, peer):
        return pltpu.make_async_remote_copy(
            src_ref=stage.at[k * 3 + d, slot],
            dst_ref=renorm_ref.at[source * ops + k, :, pl.ds(d * kept, kept)],
            send_sem=send_sem.at[k * 3 + d, slot], recv_sem=recv_sem.at[k * 3 + d, source],
            device_id=(sec, peer), device_id_type=MESH,
        )

    def cut(target, value, count, each):
        if each % 16 == 0:
            for p in range(count):
                target[p] = value[p * each : (p + 1) * each].astype(jnp.bfloat16)
        else:
            full[:, : value.shape[1]] = value
            for p in range(count):
                target[p] = full[pl.ds(p * each, each), : value.shape[1]].astype(jnp.bfloat16)

    def renorm(k, d):
        vmatrix = jnp.dot(
            left[k, :, d * row_count : (d + 1) * row_count], near_basis[d],
            preferred_element_type=jnp.float32,
        ).astype(jnp.bfloat16)
        value = jnp.dot(basis_t[...], vmatrix, preferred_element_type=jnp.float32)
        cut(stage.at[k * 3 + d], value, op_n, share)

        def send(step, carry):
            peer = lax.rem(op + step, op_n)
            piece(k, d, op, peer, peer).start()
            return carry

        lax.fori_loop(1, op_n, send, 0)
        renorm_ref[op * ops + k, :, d * kept : (d + 1) * kept] = stage[k * 3 + d, op]

    for k in range(ops):
        loads[1 + k].wait()
        renorm(k, 1)
    for d in (0, 2):
        @pl.when(has[d])
        def _():
            arrival(near_basis, 0, d).wait_recv()
            for k in range(ops):
                renorm(k, d)

        @pl.when(jnp.logical_not(has[d]))
        def _():
            def clear(g, carry):
                renorm_ref[g, :, d * kept : (d + 1) * kept] = jnp.zeros((share, kept), jnp.bfloat16)
                return carry

            lax.fori_loop(0, op_n * ops, clear, 0)

    loads[2 + ops].wait()

    def sigma_term(k, d):
        product = jnp.dot(
            left[k, :, d * row_count : (d + 1) * row_count], near_psi[d],
            preferred_element_type=jnp.float32,
        ).astype(jnp.bfloat16)
        return lax.dot_general(
            product, right[k, d], (((1,), (1,)), ((), ())), preferred_element_type=jnp.float32
        )

    total[...] = sum(sigma_term(k, 1) for k in range(ops))
    for d in (0, 2):
        @pl.when(has[d])
        def _():
            arrival(near_psi, 1, d).wait_recv()
            total[...] += sum(sigma_term(k, d) for k in range(ops))

    cut(sigma_stage, jnp.where(live_state, total[...], 0.0), op_n, sigma_share)

    def sigma_piece(source, slot, peer):
        return pltpu.make_async_remote_copy(
            src_ref=sigma_stage.at[slot], dst_ref=sigma_parts.at[source],
            send_sem=sigma_send.at[slot], recv_sem=sigma_recv.at[source],
            device_id=(sec, peer), device_id_type=MESH,
        )

    def sigma_start(step, carry):
        peer = lax.rem(op + step, op_n)
        sigma_piece(op, peer, peer).start()
        return carry

    lax.fori_loop(1, op_n, sigma_start, 0)
    total[:sigma_share] = sigma_stage[op].astype(jnp.float32)

    def sigma_add(step, carry):
        source = lax.rem(op + op_n - step, op_n)
        sigma_piece(source, source, source).wait_recv()
        total[:sigma_share] += sigma_parts[source].astype(jnp.float32)
        return carry

    lax.fori_loop(1, op_n, sigma_add, 0)
    sigma_ref[...] = total[:sigma_share].astype(jnp.bfloat16)

    def finish(k, d):
        def one(step, carry):
            source = lax.rem(op + op_n - step, op_n)
            piece(k, d, source, source, source).wait()
            return carry

        lax.fori_loop(1, op_n, one, 0)

    for k in range(ops):
        finish(k, 1)
    for d in (0, 2):
        @pl.when(has[d])
        def _():
            halo(near_basis, 0, d).wait_send()
            halo(near_psi, 1, d).wait_send()
            for k in range(ops):
                finish(k, d)

    def sigma_sent(step, carry):
        peer = lax.rem(op + step, op_n)
        sigma_piece(op, peer, peer).wait_send()
        return carry

    lax.fori_loop(1, op_n, sigma_sent, 0)


def local(sec_n, op_n, psi_blocks, sector_rows, kept_cols, basis, left_ops, right_ops):
    row_count, width = psi_blocks.shape
    kept = basis.shape[1]
    ops = left_ops.shape[0]
    share = kept // op_n
    sigma_share = row_count // op_n
    bf16 = jnp.bfloat16
    vmem = pl.BlockSpec(memory_space=pltpu.VMEM)
    smem = pl.BlockSpec(memory_space=pltpu.SMEM)
    hbm = pl.BlockSpec(memory_space=pl.ANY)
    dma = pltpu.SemaphoreType.DMA
    return pl.pallas_call(
        functools.partial(kernel, sec_n, op_n),
        out_shape=(
            jax.ShapeDtypeStruct((sigma_share, width), bf16),
            jax.ShapeDtypeStruct((ops * op_n, share, 3 * kept), bf16),
        ),
        in_specs=[smem, smem, hbm, hbm, hbm, hbm],
        out_specs=(vmem, vmem),
        scratch_shapes=[
            pltpu.VMEM((row_count, width), bf16),
            pltpu.VMEM((row_count, kept), bf16),
            pltpu.VMEM((3, row_count, width), bf16),
            pltpu.VMEM((3, row_count, kept), bf16),
            pltpu.VMEM((kept, row_count), bf16),
            pltpu.VMEM((ops, row_count, 3 * row_count), bf16),
            pltpu.VMEM((ops, 3, width, width), bf16),
            pltpu.VMEM((max(row_count, kept), max(width, kept)), jnp.float32),
            pltpu.VMEM((ops * 3, op_n, share, kept), bf16),
            pltpu.VMEM((row_count, width), jnp.float32),
            pltpu.VMEM((op_n, sigma_share, width), bf16),
            pltpu.VMEM((op_n, sigma_share, width), bf16),
            dma((ops + 3,)),
            dma((2, 3)),
            dma((2, 3)),
            dma((ops * 3, op_n)),
            dma((ops * 3, op_n)),
            dma((op_n,)),
            dma((op_n,)),
        ],
        compiler_params=pltpu.CompilerParams(
            collective_id=0, has_side_effects=True, vmem_limit_bytes=56 * 1024 * 1024
        ),
    )(sector_rows, kept_cols, psi_blocks, basis, left_ops, right_ops[:, 0])


def solution(mesh):
    placed = (
        P("sec", None),
        P("sec"),
        P("sec"),
        P("sec", None),
        P("op", "sec", None),
        P("op", "sec", None, None, None),
    )
    return jax.shard_map(
        functools.partial(local, mesh.shape["sec"], mesh.shape["op"]),
        mesh=mesh,
        in_specs=placed,
        out_specs=(P(("sec", "op"), None), P(None, ("sec", "op"), None)),
        check_vma=False,
    )
```

```python
import functools

import jax
import jax.numpy as jnp
from jax import lax
from jax.experimental import pallas as pl
from jax.experimental.pallas import tpu as pltpu
from jax.sharding import PartitionSpec as P

MESH = pl.DeviceIdType.MESH


def kernel(
    sec_n, op_n, rows_ref, cols_ref, psi_hbm, basis_hbm, left_hbm, right_hbm,
    sigma_ref, renorm_ref,
    psi_raw, basis_raw, near_psi, near_basis, basis_t, left, right, full, stage,
    total, sums, arrived, last,
    load_sem, halo_send, halo_recv, send_sem, recv_sem, sigma_send, sigma_recv,
):
    ops, row_count, _ = left.shape
    kept = basis_raw.shape[1]
    width = psi_raw.shape[1]
    share = stage.shape[2]
    sigma_share = sums.shape[1]
    sec = lax.axis_index("sec")
    op = lax.axis_index("op")
    has = (sec > 0, None, sec < sec_n - 1)

    loads = [pltpu.make_async_copy(basis_hbm, basis_raw, load_sem.at[0])]
    loads += [pltpu.make_async_copy(left_hbm.at[k], left.at[k], load_sem.at[1 + k]) for k in range(ops)]
    loads += [
        pltpu.make_async_copy(psi_hbm, psi_raw, load_sem.at[1 + ops]),
        pltpu.make_async_copy(right_hbm, right, load_sem.at[2 + ops]),
    ]
    for load in loads:
        load.start()

    barrier = pltpu.get_barrier_semaphore()

    def greet(step, carry):
        pl.semaphore_signal(
            barrier, inc=1, device_id=(sec, lax.rem(op + step, op_n)), device_id_type=MESH
        )
        return carry

    for d in (0, 2):
        @pl.when(has[d])
        def _():
            pl.semaphore_signal(barrier, inc=1, device_id=(sec + d - 1, op), device_id_type=MESH)
    lax.fori_loop(1, op_n, greet, 0)

    live = lax.broadcasted_iota(jnp.int32, (row_count, kept), 0) < rows_ref[0]
    live_kept = live & (lax.broadcasted_iota(jnp.int32, (row_count, kept), 1) < cols_ref[0])
    loads[0].wait()
    masked = jnp.where(live_kept, basis_raw[...].astype(jnp.float32), 0.0)
    near_basis[1] = masked.astype(jnp.bfloat16)
    live_state = lax.broadcasted_iota(jnp.int32, (row_count, width), 0) < rows_ref[0]
    loads[1 + ops].wait()
    near_psi[1] = jnp.where(live_state, psi_raw[...].astype(jnp.float32), 0.0).astype(jnp.bfloat16)

    beside = (sec > 0).astype(jnp.int32) + (sec < sec_n - 1).astype(jnp.int32)
    pl.semaphore_wait(barrier, op_n - 1 + beside)

    def halo(near, at, d):
        return pltpu.make_async_remote_copy(
            src_ref=near.at[1], dst_ref=near.at[2 - d],
            send_sem=halo_send.at[at, d], recv_sem=halo_recv.at[at, 2 - d],
            device_id=(sec + d - 1, op), device_id_type=MESH,
        )

    def arrival(near, at, d):
        return pltpu.make_async_remote_copy(
            src_ref=near.at[1], dst_ref=near.at[d],
            send_sem=halo_send.at[at, d], recv_sem=halo_recv.at[at, d],
            device_id=(sec + d - 1, op), device_id_type=MESH,
        )

    for at, near in ((0, near_basis), (1, near_psi)):
        for d in (0, 2):
            @pl.when(has[d])
            def _():
                halo(near, at, d).start()

    basis_t[...] = masked.T.astype(jnp.bfloat16)

    def piece(k, d, source, slot, peer):
        return pltpu.make_async_remote_copy(
            src_ref=stage.at[k * 3 + d, slot],
            dst_ref=renorm_ref.at[source * ops + k, :, pl.ds(d * kept, kept)],
            send_sem=send_sem.at[k * 3 + d, slot], recv_sem=recv_sem.at[k * 3 + d, source],
            device_id=(sec, peer), device_id_type=MESH,
        )

    def cut(target, value, count, each):
        if each % 16 == 0:
            for p in range(count):
                target[p] = value[p * each : (p + 1) * each].astype(target.dtype)
        else:
            full[:, : value.shape[1]] = value
            for p in range(count):
                target[p] = full[pl.ds(p * each, each), : value.shape[1]].astype(target.dtype)

    def renorm(k, d):
        vmatrix = jnp.dot(
            left[k, :, d * row_count : (d + 1) * row_count], near_basis[d],
            preferred_element_type=jnp.float32,
        ).astype(jnp.bfloat16)
        value = jnp.dot(basis_t[...], vmatrix, preferred_element_type=jnp.float32)
        cut(stage.at[k * 3 + d], value, op_n, share)

        def send(step, carry):
            peer = lax.rem(op + step, op_n)
            piece(k, d, op, peer, peer).start()
            return carry

        lax.fori_loop(1, op_n, send, 0)
        renorm_ref[op * ops + k, :, d * kept : (d + 1) * kept] = stage[k * 3 + d, op]

    for k in range(ops):
        loads[1 + k].wait()
        renorm(k, 1)
    def side(d):
        @pl.when(has[d])
        def _():
            arrival(near_basis, 0, d).wait_recv()
            for k in range(ops):
                renorm(k, d)

        @pl.when(jnp.logical_not(has[d]))
        def _():
            def clear(g, carry):
                renorm_ref[g, :, d * kept : (d + 1) * kept] = jnp.zeros((share, kept), jnp.bfloat16)
                return carry

            lax.fori_loop(0, op_n * ops, clear, 0)

    loads[2 + ops].wait()

    def sigma_term(k, d):
        product = jnp.dot(
            left[k, :, d * row_count : (d + 1) * row_count], near_psi[d],
            preferred_element_type=jnp.float32,
        ).astype(jnp.bfloat16)
        return lax.dot_general(
            product, right[k, d], (((1,), (1,)), ((), ())), preferred_element_type=jnp.float32
        )

    total[...] = sum(sigma_term(k, 1) for k in range(ops))
    for d in (0, 2):
        @pl.when(has[d])
        def _():
            arrival(near_psi, 1, d).wait_recv()
            total[...] += sum(sigma_term(k, d) for k in range(ops))

    cut(sums, jnp.where(live_state, total[...], 0.0), op_n, sigma_share)

    levels = op_n.bit_length() - 1

    def partner(level):
        return op + (1 - 2 * (op // 2**level % 2)) * 2**level

    def sigma_piece(level, j, mine):
        low = op % 2**level
        here, there = op // 2**level % 2, partner(level) // 2**level % 2
        owner = low + (here if mine else there) * 2**level + j * 2 ** (level + 1)
        slot = op_n - op_n // 2**level + j
        if level == levels - 1:
            source, target = last.at[0], last.at[1]
        else:
            source, target = sums.at[owner], arrived.at[slot]
        return owner, pltpu.make_async_remote_copy(
            src_ref=source, dst_ref=target,
            send_sem=sigma_send.at[slot], recv_sem=sigma_recv.at[slot],
            device_id=(sec, partner(level)), device_id_type=MESH,
        )

    def sigma_start(level):
        for j in range(op_n // 2 ** (level + 1)):
            owner, copy = sigma_piece(level, j, False)
            if level == levels - 1:
                last[0] = sums[owner].astype(jnp.bfloat16)
            copy.start()

    def sigma_add(level):
        for j in range(op_n // 2 ** (level + 1)):
            owner, copy = sigma_piece(level, j, True)
            copy.wait_recv()
            slot = op_n - op_n // 2**level + j
            if level == levels - 1:
                sigma_ref[...] = (sums[owner] + last[1].astype(jnp.float32)).astype(jnp.bfloat16)
            else:
                sums[owner] += arrived[slot]

    sigma_start(0)
    side(0)
    sigma_add(0)
    sigma_start(1)
    side(2)
    for level in range(1, levels):
        sigma_add(level)
        if level + 1 < levels:
            sigma_start(level + 1)

    def finish(k, d):
        def one(step, carry):
            source = lax.rem(op + op_n - step, op_n)
            piece(k, d, source, source, source).wait()
            return carry

        lax.fori_loop(1, op_n, one, 0)

    for k in range(ops):
        finish(k, 1)
    for d in (0, 2):
        @pl.when(has[d])
        def _():
            halo(near_basis, 0, d).wait_send()
            halo(near_psi, 1, d).wait_send()
            for k in range(ops):
                finish(k, d)

    for level in range(levels):
        for j in range(op_n // 2 ** (level + 1)):
            sigma_piece(level, j, False)[1].wait_send()


def local(sec_n, op_n, psi_blocks, sector_rows, kept_cols, basis, left_ops, right_ops):
    row_count, width = psi_blocks.shape
    kept = basis.shape[1]
    ops = left_ops.shape[0]
    share = kept // op_n
    sigma_share = row_count // op_n
    bf16 = jnp.bfloat16
    vmem = pl.BlockSpec(memory_space=pltpu.VMEM)
    smem = pl.BlockSpec(memory_space=pltpu.SMEM)
    hbm = pl.BlockSpec(memory_space=pl.ANY)
    dma = pltpu.SemaphoreType.DMA
    return pl.pallas_call(
        functools.partial(kernel, sec_n, op_n),
        out_shape=(
            jax.ShapeDtypeStruct((sigma_share, width), bf16),
            jax.ShapeDtypeStruct((ops * op_n, share, 3 * kept), bf16),
        ),
        in_specs=[smem, smem, hbm, hbm, hbm, hbm],
        out_specs=(vmem, vmem),
        scratch_shapes=[
            pltpu.VMEM((row_count, width), bf16),
            pltpu.VMEM((row_count, kept), bf16),
            pltpu.VMEM((3, row_count, width), bf16),
            pltpu.VMEM((3, row_count, kept), bf16),
            pltpu.VMEM((kept, row_count), bf16),
            pltpu.VMEM((ops, row_count, 3 * row_count), bf16),
            pltpu.VMEM((ops, 3, width, width), bf16),
            pltpu.VMEM((max(row_count, kept), max(width, kept)), jnp.float32),
            pltpu.VMEM((ops * 3, op_n, share, kept), bf16),
            pltpu.VMEM((row_count, width), jnp.float32),
            pltpu.VMEM((op_n, sigma_share, width), jnp.float32),
            pltpu.VMEM((op_n, sigma_share, width), jnp.float32),
            pltpu.VMEM((2, sigma_share, width), bf16),
            dma((ops + 3,)),
            dma((2, 3)),
            dma((2, 3)),
            dma((ops * 3, op_n)),
            dma((ops * 3, op_n)),
            dma((op_n,)),
            dma((op_n,)),
        ],
        compiler_params=pltpu.CompilerParams(
            collective_id=0, has_side_effects=True, vmem_limit_bytes=56 * 1024 * 1024
        ),
    )(sector_rows, kept_cols, psi_blocks, basis, left_ops, right_ops[:, 0])


def solution(mesh):
    placed = (
        P("sec", None),
        P("sec"),
        P("sec"),
        P("sec", None),
        P("op", "sec", None),
        P("op", "sec", None, None, None),
    )
    return jax.shard_map(
        functools.partial(local, mesh.shape["sec"], mesh.shape["op"]),
        mesh=mesh,
        in_specs=placed,
        out_specs=(P(("sec", "op"), None), P(None, ("sec", "op"), None)),
        check_vma=False,
    )
```

```python
import functools

import jax
import jax.numpy as jnp
from jax import lax
from jax.experimental import pallas as pl
from jax.experimental.pallas import tpu as pltpu
from jax.sharding import PartitionSpec as P

MESH = pl.DeviceIdType.MESH


def kernel(
    sec_n, op_n, rows_ref, cols_ref, psi_hbm, basis_hbm, left_hbm, right_hbm,
    sigma_ref, renorm_ref,
    psi_raw, basis_raw, near_psi, near_basis, basis_t, left, right, full, stage,
    total, sums, arrived, last,
    load_sem, halo_send, halo_recv, send_sem, recv_sem, sigma_send, sigma_recv,
):
    ops, row_count, _ = left.shape
    kept = basis_raw.shape[1]
    width = psi_raw.shape[1]
    share = stage.shape[2]
    sigma_share = sums.shape[1]
    sec = lax.axis_index("sec")
    op = lax.axis_index("op")
    has = (sec > 0, None, sec < sec_n - 1)

    loads = [pltpu.make_async_copy(basis_hbm, basis_raw, load_sem.at[0])]
    loads += [pltpu.make_async_copy(left_hbm.at[k], left.at[k], load_sem.at[1 + k]) for k in range(ops)]
    loads += [
        pltpu.make_async_copy(psi_hbm, psi_raw, load_sem.at[1 + ops]),
        pltpu.make_async_copy(right_hbm, right, load_sem.at[2 + ops]),
    ]
    for load in loads:
        load.start()

    barrier = pltpu.get_barrier_semaphore()

    def greet(step, carry):
        pl.semaphore_signal(
            barrier, inc=1, device_id=(sec, lax.rem(op + step, op_n)), device_id_type=MESH
        )
        return carry

    for d in (0, 2):
        @pl.when(has[d])
        def _():
            pl.semaphore_signal(barrier, inc=1, device_id=(sec + d - 1, op), device_id_type=MESH)
    lax.fori_loop(1, op_n, greet, 0)

    live = lax.broadcasted_iota(jnp.int32, (row_count, kept), 0) < rows_ref[0]
    live_kept = live & (lax.broadcasted_iota(jnp.int32, (row_count, kept), 1) < cols_ref[0])
    loads[0].wait()
    masked = jnp.where(live_kept, basis_raw[...].astype(jnp.float32), 0.0)
    near_basis[1] = masked.astype(jnp.bfloat16)
    live_state = lax.broadcasted_iota(jnp.int32, (row_count, width), 0) < rows_ref[0]
    loads[1 + ops].wait()
    near_psi[1] = jnp.where(live_state, psi_raw[...].astype(jnp.float32), 0.0).astype(jnp.bfloat16)

    beside = (sec > 0).astype(jnp.int32) + (sec < sec_n - 1).astype(jnp.int32)
    pl.semaphore_wait(barrier, op_n - 1 + beside)

    def halo(near, at, d):
        return pltpu.make_async_remote_copy(
            src_ref=near.at[1], dst_ref=near.at[2 - d],
            send_sem=halo_send.at[at, d], recv_sem=halo_recv.at[at, 2 - d],
            device_id=(sec + d - 1, op), device_id_type=MESH,
        )

    def arrival(near, at, d):
        return pltpu.make_async_remote_copy(
            src_ref=near.at[1], dst_ref=near.at[d],
            send_sem=halo_send.at[at, d], recv_sem=halo_recv.at[at, d],
            device_id=(sec + d - 1, op), device_id_type=MESH,
        )

    for at, near in ((0, near_basis), (1, near_psi)):
        for d in (0, 2):
            @pl.when(has[d])
            def _():
                halo(near, at, d).start()

    basis_t[...] = masked.T.astype(jnp.bfloat16)

    def piece(k, d, source, slot, peer):
        return pltpu.make_async_remote_copy(
            src_ref=stage.at[k * 3 + d, slot],
            dst_ref=renorm_ref.at[source * ops + k, :, pl.ds(d * kept, kept)],
            send_sem=send_sem.at[k * 3 + d, slot], recv_sem=recv_sem.at[k * 3 + d, source],
            device_id=(sec, peer), device_id_type=MESH,
        )

    def cut(target, value, count, each):
        if each % 16 == 0:
            for p in range(count):
                target[p] = value[p * each : (p + 1) * each].astype(target.dtype)
        else:
            full[:, : value.shape[1]] = value
            for p in range(count):
                target[p] = full[pl.ds(p * each, each), : value.shape[1]].astype(target.dtype)

    def renorm(k, d):
        vmatrix = jnp.dot(
            left[k, :, d * row_count : (d + 1) * row_count], near_basis[d],
            preferred_element_type=jnp.float32,
        ).astype(jnp.bfloat16)
        value = jnp.dot(basis_t[...], vmatrix, preferred_element_type=jnp.float32)
        cut(stage.at[k * 3 + d], value, op_n, share)

        def send(step, carry):
            peer = lax.rem(op + step, op_n)
            piece(k, d, op, peer, peer).start()
            return carry

        lax.fori_loop(1, op_n, send, 0)
        renorm_ref[op * ops + k, :, d * kept : (d + 1) * kept] = stage[k * 3 + d, op]

    for k in range(ops):
        loads[1 + k].wait()
        renorm(k, 1)
    def side(d):
        @pl.when(has[d])
        def _():
            arrival(near_basis, 0, d).wait_recv()
            for k in range(ops):
                renorm(k, d)

        @pl.when(jnp.logical_not(has[d]))
        def _():
            def clear(g, carry):
                renorm_ref[g, :, d * kept : (d + 1) * kept] = jnp.zeros((share, kept), jnp.bfloat16)
                return carry

            lax.fori_loop(0, op_n * ops, clear, 0)

    loads[2 + ops].wait()

    def sigma_term(k, d):
        product = jnp.dot(
            left[k, :, d * row_count : (d + 1) * row_count], near_psi[d],
            preferred_element_type=jnp.float32,
        ).astype(jnp.bfloat16)
        return lax.dot_general(
            product, right[k, d], (((1,), (1,)), ((), ())), preferred_element_type=jnp.float32
        )

    total[...] = sum(sigma_term(k, 1) for k in range(ops))
    for d in (0, 2):
        @pl.when(has[d])
        def _():
            arrival(near_psi, 1, d).wait_recv()
            total[...] += sum(sigma_term(k, d) for k in range(ops))

    cut(sums, jnp.where(live_state, total[...], 0.0), op_n, sigma_share)

    levels = op_n.bit_length() - 1

    def partner(level):
        return op + (1 - 2 * (op // 2**level % 2)) * 2**level

    def sigma_piece(level, j, mine):
        low = op % 2**level
        here, there = op // 2**level % 2, partner(level) // 2**level % 2
        owner = low + (here if mine else there) * 2**level + j * 2 ** (level + 1)
        slot = op_n - op_n // 2**level + j
        if level == levels - 1:
            source, target = last.at[0], last.at[1]
        else:
            source, target = sums.at[owner], arrived.at[slot]
        return owner, pltpu.make_async_remote_copy(
            src_ref=source, dst_ref=target,
            send_sem=sigma_send.at[slot], recv_sem=sigma_recv.at[slot],
            device_id=(sec, partner(level)), device_id_type=MESH,
        )

    def sigma_start(level):
        for j in range(op_n // 2 ** (level + 1)):
            owner, copy = sigma_piece(level, j, False)
            if level == levels - 1:
                last[0] = sums[owner].astype(jnp.bfloat16)
            copy.start()

    def sigma_add(level):
        for j in range(op_n // 2 ** (level + 1)):
            owner, copy = sigma_piece(level, j, True)
            copy.wait_recv()
            slot = op_n - op_n // 2**level + j
            if level == levels - 1:
                sigma_ref[...] = (sums[owner] + last[1].astype(jnp.float32)).astype(jnp.bfloat16)
            else:
                sums[owner] += arrived[slot]

    sigma_start(0)
    side(0)
    sigma_add(0)
    sigma_start(1)
    side(2)
    for level in range(1, levels):
        sigma_add(level)
        if level + 1 < levels:
            sigma_start(level + 1)

    def finish(k, d):
        def one(step, carry):
            source = lax.rem(op + op_n - step, op_n)
            piece(k, d, source, source, source).wait()
            return carry

        lax.fori_loop(1, op_n, one, 0)

    for k in range(ops):
        finish(k, 1)
    for d in (0, 2):
        @pl.when(has[d])
        def _():
            halo(near_basis, 0, d).wait_send()
            halo(near_psi, 1, d).wait_send()
            for k in range(ops):
                finish(k, d)

    for level in range(levels):
        for j in range(op_n // 2 ** (level + 1)):
            sigma_piece(level, j, False)[1].wait_send()


def deliver(sigma_in, renorm_in, sigma_out, renorm_out, sem):
    copies = (
        pltpu.make_async_copy(sigma_in, sigma_out, sem.at[0]),
        pltpu.make_async_copy(renorm_in, renorm_out, sem.at[1]),
    )
    for copy in copies:
        copy.start()
    for copy in copies:
        copy.wait()


def local(sec_n, op_n, psi_blocks, sector_rows, kept_cols, basis, left_ops, right_ops):
    row_count, width = psi_blocks.shape
    kept = basis.shape[1]
    ops = left_ops.shape[0]
    share = kept // op_n
    sigma_share = row_count // op_n
    bf16 = jnp.bfloat16
    vmem = pl.BlockSpec(memory_space=pltpu.VMEM)
    smem = pl.BlockSpec(memory_space=pltpu.SMEM)
    hbm = pl.BlockSpec(memory_space=pl.ANY)
    dma = pltpu.SemaphoreType.DMA
    results = (
        jax.ShapeDtypeStruct((sigma_share, width), bf16),
        jax.ShapeDtypeStruct((ops * op_n, share, 3 * kept), bf16),
    )
    made = pl.pallas_call(
        functools.partial(kernel, sec_n, op_n),
        out_shape=tuple(pltpu.VMEM(x.shape, x.dtype) for x in results),
        in_specs=[smem, smem, hbm, hbm, hbm, hbm],
        out_specs=(vmem, vmem),
        scratch_shapes=[
            pltpu.VMEM((row_count, width), bf16),
            pltpu.VMEM((row_count, kept), bf16),
            pltpu.VMEM((3, row_count, width), bf16),
            pltpu.VMEM((3, row_count, kept), bf16),
            pltpu.VMEM((kept, row_count), bf16),
            pltpu.VMEM((ops, row_count, 3 * row_count), bf16),
            pltpu.VMEM((ops, 3, width, width), bf16),
            pltpu.VMEM((max(row_count, kept), max(width, kept)), jnp.float32),
            pltpu.VMEM((ops * 3, op_n, share, kept), bf16),
            pltpu.VMEM((row_count, width), jnp.float32),
            pltpu.VMEM((op_n, sigma_share, width), jnp.float32),
            pltpu.VMEM((op_n, sigma_share, width), jnp.float32),
            pltpu.VMEM((2, sigma_share, width), bf16),
            dma((ops + 3,)),
            dma((2, 3)),
            dma((2, 3)),
            dma((ops * 3, op_n)),
            dma((ops * 3, op_n)),
            dma((op_n,)),
            dma((op_n,)),
        ],
        compiler_params=pltpu.CompilerParams(
            collective_id=0, has_side_effects=True, vmem_limit_bytes=56 * 1024 * 1024
        ),
    )(sector_rows, kept_cols, psi_blocks, basis, left_ops, right_ops[:, 0])
    return pl.pallas_call(
        deliver,
        out_shape=results,
        in_specs=[hbm, hbm],
        out_specs=(hbm, hbm),
        scratch_shapes=[dma((2,))],
        compiler_params=pltpu.CompilerParams(vmem_limit_bytes=1024 * 1024),
    )(*made)


def solution(mesh):
    placed = (
        P("sec", None),
        P("sec"),
        P("sec"),
        P("sec", None),
        P("op", "sec", None),
        P("op", "sec", None, None, None),
    )
    return jax.shard_map(
        functools.partial(local, mesh.shape["sec"], mesh.shape["op"]),
        mesh=mesh,
        in_specs=placed,
        out_specs=(P(("sec", "op"), None), P(None, ("sec", "op"), None)),
        check_vma=False,
    )
```

```python
import functools

import jax
import jax.numpy as jnp
from jax import lax
from jax.experimental import pallas as pl
from jax.experimental.pallas import tpu as pltpu
from jax.sharding import PartitionSpec as P

MESH = pl.DeviceIdType.MESH


def kernel(
    sec_n, op_n, rows_ref, cols_ref, psi_hbm, basis_hbm, left_hbm, right_hbm,
    sigma_ref, renorm_ref,
    psi_raw, basis_raw, near_psi, near_basis, basis_t, left, right, full, stage,
    total, sums, arrived, last,
    load_sem, halo_send, halo_recv, send_sem, recv_sem, sigma_send, sigma_recv,
):
    ops, row_count, _ = left.shape
    kept = basis_raw.shape[1]
    width = psi_raw.shape[1]
    share = stage.shape[2]
    sigma_share = sums.shape[1]
    sec = lax.axis_index("sec")
    op = lax.axis_index("op")
    has = (sec > 0, None, sec < sec_n - 1)

    loads = [pltpu.make_async_copy(basis_hbm, basis_raw, load_sem.at[0])]
    loads += [pltpu.make_async_copy(left_hbm.at[k], left.at[k], load_sem.at[1 + k]) for k in range(ops)]
    loads += [
        pltpu.make_async_copy(psi_hbm, psi_raw, load_sem.at[1 + ops]),
        pltpu.make_async_copy(right_hbm, right, load_sem.at[2 + ops]),
    ]
    for load in loads:
        load.start()

    barrier = pltpu.get_barrier_semaphore()

    def greet(step, carry):
        pl.semaphore_signal(
            barrier, inc=1, device_id=(sec, lax.rem(op + step, op_n)), device_id_type=MESH
        )
        return carry

    for d in (0, 2):
        @pl.when(has[d])
        def _():
            pl.semaphore_signal(barrier, inc=1, device_id=(sec + d - 1, op), device_id_type=MESH)
    lax.fori_loop(1, op_n, greet, 0)

    live = lax.broadcasted_iota(jnp.int32, (row_count, kept), 0) < rows_ref[0]
    live_kept = live & (lax.broadcasted_iota(jnp.int32, (row_count, kept), 1) < cols_ref[0])
    loads[0].wait()
    masked = jnp.where(live_kept, basis_raw[...].astype(jnp.float32), 0.0)
    near_basis[1] = masked.astype(jnp.bfloat16)
    live_state = lax.broadcasted_iota(jnp.int32, (row_count, width), 0) < rows_ref[0]
    loads[1 + ops].wait()
    near_psi[1] = jnp.where(live_state, psi_raw[...].astype(jnp.float32), 0.0).astype(jnp.bfloat16)

    beside = (sec > 0).astype(jnp.int32) + (sec < sec_n - 1).astype(jnp.int32)
    pl.semaphore_wait(barrier, op_n - 1 + beside)

    def halo(near, at, d):
        return pltpu.make_async_remote_copy(
            src_ref=near.at[1], dst_ref=near.at[2 - d],
            send_sem=halo_send.at[at, d], recv_sem=halo_recv.at[at, 2 - d],
            device_id=(sec + d - 1, op), device_id_type=MESH,
        )

    def arrival(near, at, d):
        return pltpu.make_async_remote_copy(
            src_ref=near.at[1], dst_ref=near.at[d],
            send_sem=halo_send.at[at, d], recv_sem=halo_recv.at[at, d],
            device_id=(sec + d - 1, op), device_id_type=MESH,
        )

    for at, near in ((0, near_basis), (1, near_psi)):
        for d in (0, 2):
            @pl.when(has[d])
            def _():
                halo(near, at, d).start()

    basis_t[...] = masked.T.astype(jnp.bfloat16)

    def piece(k, d, source, slot, peer):
        return pltpu.make_async_remote_copy(
            src_ref=stage.at[k * 3 + d, slot],
            dst_ref=renorm_ref.at[source * ops + k, :, pl.ds(d * kept, kept)],
            send_sem=send_sem.at[k * 3 + d, slot], recv_sem=recv_sem.at[k * 3 + d, source],
            device_id=(sec, peer), device_id_type=MESH,
        )

    def cut(target, value, count, each):
        if each % 16 == 0:
            for p in range(count):
                target[p] = value[p * each : (p + 1) * each].astype(target.dtype)
        else:
            full[:, : value.shape[1]] = value
            for p in range(count):
                target[p] = full[pl.ds(p * each, each), : value.shape[1]].astype(target.dtype)

    def renorm(k, d):
        vmatrix = jnp.dot(
            left[k, :, d * row_count : (d + 1) * row_count], near_basis[d],
            preferred_element_type=jnp.float32,
        ).astype(jnp.bfloat16)
        value = jnp.dot(basis_t[...], vmatrix, preferred_element_type=jnp.float32)
        cut(stage.at[k * 3 + d], value, op_n, share)

        def send(step, carry):
            peer = lax.rem(op + 1 + lax.rem(step - 1 + op, op_n - 1), op_n)
            piece(k, d, op, peer, peer).start()
            return carry

        lax.fori_loop(1, op_n, send, 0)
        renorm_ref[op * ops + k, :, d * kept : (d + 1) * kept] = stage[k * 3 + d, op]

    for k in range(ops):
        loads[1 + k].wait()
        renorm(k, 1)
    def side(d):
        @pl.when(has[d])
        def _():
            arrival(near_basis, 0, d).wait_recv()
            for k in range(ops):
                renorm(k, d)

        @pl.when(jnp.logical_not(has[d]))
        def _():
            def clear(g, carry):
                renorm_ref[g, :, d * kept : (d + 1) * kept] = jnp.zeros((share, kept), jnp.bfloat16)
                return carry

            lax.fori_loop(0, op_n * ops, clear, 0)

    loads[2 + ops].wait()

    def sigma_term(k, d):
        product = jnp.dot(
            left[k, :, d * row_count : (d + 1) * row_count], near_psi[d],
            preferred_element_type=jnp.float32,
        ).astype(jnp.bfloat16)
        return lax.dot_general(
            product, right[k, d], (((1,), (1,)), ((), ())), preferred_element_type=jnp.float32
        )

    total[...] = sum(sigma_term(k, 1) for k in range(ops))
    for d in (0, 2):
        @pl.when(has[d])
        def _():
            arrival(near_psi, 1, d).wait_recv()
            total[...] += sum(sigma_term(k, d) for k in range(ops))

    cut(sums, jnp.where(live_state, total[...], 0.0), op_n, sigma_share)

    levels = op_n.bit_length() - 1

    def partner(level):
        return op + (1 - 2 * (op // 2**level % 2)) * 2**level

    def sigma_piece(level, j, mine):
        low = op % 2**level
        here, there = op // 2**level % 2, partner(level) // 2**level % 2
        owner = low + (here if mine else there) * 2**level + j * 2 ** (level + 1)
        slot = op_n - op_n // 2**level + j
        if level == levels - 1:
            source, target = last.at[0], last.at[1]
        else:
            source, target = sums.at[owner], arrived.at[slot]
        return owner, pltpu.make_async_remote_copy(
            src_ref=source, dst_ref=target,
            send_sem=sigma_send.at[slot], recv_sem=sigma_recv.at[slot],
            device_id=(sec, partner(level)), device_id_type=MESH,
        )

    def sigma_start(level):
        for j in range(op_n // 2 ** (level + 1)):
            owner, copy = sigma_piece(level, j, False)
            if level == levels - 1:
                last[0] = sums[owner].astype(jnp.bfloat16)
            copy.start()

    def sigma_add(level):
        for j in range(op_n // 2 ** (level + 1)):
            owner, copy = sigma_piece(level, j, True)
            copy.wait_recv()
            slot = op_n - op_n // 2**level + j
            if level == levels - 1:
                sigma_ref[...] = (sums[owner] + last[1].astype(jnp.float32)).astype(jnp.bfloat16)
            else:
                sums[owner] += arrived[slot]

    sigma_start(0)
    side(0)
    sigma_add(0)
    sigma_start(1)
    side(2)
    for level in range(1, levels):
        sigma_add(level)
        if level + 1 < levels:
            sigma_start(level + 1)

    def finish(k, d):
        def one(step, carry):
            source = lax.rem(op + op_n - step, op_n)
            piece(k, d, source, source, source).wait()
            return carry

        lax.fori_loop(1, op_n, one, 0)

    for k in range(ops):
        finish(k, 1)
    for d in (0, 2):
        @pl.when(has[d])
        def _():
            halo(near_basis, 0, d).wait_send()
            halo(near_psi, 1, d).wait_send()
            for k in range(ops):
                finish(k, d)

    for level in range(levels):
        for j in range(op_n // 2 ** (level + 1)):
            sigma_piece(level, j, False)[1].wait_send()


def deliver(sigma_in, renorm_in, sigma_out, renorm_out, sem):
    copies = (
        pltpu.make_async_copy(sigma_in, sigma_out, sem.at[0]),
        pltpu.make_async_copy(renorm_in, renorm_out, sem.at[1]),
    )
    for copy in copies:
        copy.start()
    for copy in copies:
        copy.wait()


def local(sec_n, op_n, psi_blocks, sector_rows, kept_cols, basis, left_ops, right_ops):
    row_count, width = psi_blocks.shape
    kept = basis.shape[1]
    ops = left_ops.shape[0]
    share = kept // op_n
    sigma_share = row_count // op_n
    bf16 = jnp.bfloat16
    vmem = pl.BlockSpec(memory_space=pltpu.VMEM)
    smem = pl.BlockSpec(memory_space=pltpu.SMEM)
    hbm = pl.BlockSpec(memory_space=pl.ANY)
    dma = pltpu.SemaphoreType.DMA
    results = (
        jax.ShapeDtypeStruct((sigma_share, width), bf16),
        jax.ShapeDtypeStruct((ops * op_n, share, 3 * kept), bf16),
    )
    made = pl.pallas_call(
        functools.partial(kernel, sec_n, op_n),
        out_shape=tuple(pltpu.VMEM(x.shape, x.dtype) for x in results),
        in_specs=[smem, smem, hbm, hbm, hbm, hbm],
        out_specs=(vmem, vmem),
        scratch_shapes=[
            pltpu.VMEM((row_count, width), bf16),
            pltpu.VMEM((row_count, kept), bf16),
            pltpu.VMEM((3, row_count, width), bf16),
            pltpu.VMEM((3, row_count, kept), bf16),
            pltpu.VMEM((kept, row_count), bf16),
            pltpu.VMEM((ops, row_count, 3 * row_count), bf16),
            pltpu.VMEM((ops, 3, width, width), bf16),
            pltpu.VMEM((max(row_count, kept), max(width, kept)), jnp.float32),
            pltpu.VMEM((ops * 3, op_n, share, kept), bf16),
            pltpu.VMEM((row_count, width), jnp.float32),
            pltpu.VMEM((op_n, sigma_share, width), jnp.float32),
            pltpu.VMEM((op_n, sigma_share, width), jnp.float32),
            pltpu.VMEM((2, sigma_share, width), bf16),
            dma((ops + 3,)),
            dma((2, 3)),
            dma((2, 3)),
            dma((ops * 3, op_n)),
            dma((ops * 3, op_n)),
            dma((op_n,)),
            dma((op_n,)),
        ],
        compiler_params=pltpu.CompilerParams(
            collective_id=0, has_side_effects=True, vmem_limit_bytes=56 * 1024 * 1024
        ),
    )(sector_rows, kept_cols, psi_blocks, basis, left_ops, right_ops[:, 0])
    return pl.pallas_call(
        deliver,
        out_shape=results,
        in_specs=[hbm, hbm],
        out_specs=(hbm, hbm),
        scratch_shapes=[dma((2,))],
        compiler_params=pltpu.CompilerParams(vmem_limit_bytes=1024 * 1024),
    )(*made)


def solution(mesh):
    placed = (
        P("sec", None),
        P("sec"),
        P("sec"),
        P("sec", None),
        P("op", "sec", None),
        P("op", "sec", None, None, None),
    )
    return jax.shard_map(
        functools.partial(local, mesh.shape["sec"], mesh.shape["op"]),
        mesh=mesh,
        in_specs=placed,
        out_specs=(P(("sec", "op"), None), P(None, ("sec", "op"), None)),
        check_vma=False,
    )
```

```python
import functools

import jax
import jax.numpy as jnp
from jax import lax
from jax.experimental import pallas as pl
from jax.experimental.pallas import tpu as pltpu
from jax.sharding import PartitionSpec as P

MESH = pl.DeviceIdType.MESH


def kernel(
    sec_n, op_n, rows_ref, cols_ref, psi_hbm, basis_hbm, left_hbm, right_hbm,
    sigma_ref, renorm_ref,
    psi_raw, basis_raw, near_psi, near_basis, basis_t, left, right, full, stage,
    total, sums, arrived, last,
    load_sem, halo_send, halo_recv, send_sem, recv_sem, sigma_send, sigma_recv,
):
    ops, row_count, _ = left.shape
    kept = basis_raw.shape[1]
    width = psi_raw.shape[1]
    share = stage.shape[2]
    sigma_share = sums.shape[1]
    sec = lax.axis_index("sec")
    op = lax.axis_index("op")
    has = (sec > 0, None, sec < sec_n - 1)

    loads = [pltpu.make_async_copy(basis_hbm, basis_raw, load_sem.at[0])]
    loads += [pltpu.make_async_copy(left_hbm.at[k], left.at[k], load_sem.at[1 + k]) for k in range(ops)]
    loads += [
        pltpu.make_async_copy(psi_hbm, psi_raw, load_sem.at[1 + ops]),
        pltpu.make_async_copy(right_hbm, right, load_sem.at[2 + ops]),
    ]
    for load in loads:
        load.start()

    barrier = pltpu.get_barrier_semaphore()

    def greet(step, carry):
        pl.semaphore_signal(
            barrier, inc=1, device_id=(sec, lax.rem(op + step, op_n)), device_id_type=MESH
        )
        return carry

    for d in (0, 2):
        @pl.when(has[d])
        def _():
            pl.semaphore_signal(barrier, inc=1, device_id=(sec + d - 1, op), device_id_type=MESH)
    lax.fori_loop(1, op_n, greet, 0)

    live = lax.broadcasted_iota(jnp.int32, (row_count, kept), 0) < rows_ref[0]
    live_kept = live & (lax.broadcasted_iota(jnp.int32, (row_count, kept), 1) < cols_ref[0])
    loads[0].wait()
    masked = jnp.where(live_kept, basis_raw[...].astype(jnp.float32), 0.0)
    near_basis[1] = masked.astype(jnp.bfloat16)
    live_state = lax.broadcasted_iota(jnp.int32, (row_count, width), 0) < rows_ref[0]
    loads[1 + ops].wait()
    near_psi[1] = jnp.where(live_state, psi_raw[...].astype(jnp.float32), 0.0).astype(jnp.bfloat16)

    beside = (sec > 0).astype(jnp.int32) + (sec < sec_n - 1).astype(jnp.int32)
    pl.semaphore_wait(barrier, op_n - 1 + beside)

    def halo(near, at, d):
        return pltpu.make_async_remote_copy(
            src_ref=near.at[1], dst_ref=near.at[2 - d],
            send_sem=halo_send.at[at, d], recv_sem=halo_recv.at[at, 2 - d],
            device_id=(sec + d - 1, op), device_id_type=MESH,
        )

    def arrival(near, at, d):
        return pltpu.make_async_remote_copy(
            src_ref=near.at[1], dst_ref=near.at[d],
            send_sem=halo_send.at[at, d], recv_sem=halo_recv.at[at, d],
            device_id=(sec + d - 1, op), device_id_type=MESH,
        )

    def halos(near, at):
        for d in (0, 2):
            @pl.when(has[d])
            def _():
                halo(near, at, d).start()

    basis_t[...] = masked.T.astype(jnp.bfloat16)

    def piece(k, d, source, slot, peer):
        return pltpu.make_async_remote_copy(
            src_ref=stage.at[k * 3 + d, slot],
            dst_ref=renorm_ref.at[source * ops + k, :, pl.ds(d * kept, kept)],
            send_sem=send_sem.at[k * 3 + d, slot], recv_sem=recv_sem.at[k * 3 + d, source],
            device_id=(sec, peer), device_id_type=MESH,
        )

    def cut(target, value, count, each):
        if each % 16 == 0:
            for p in range(count):
                target[p] = value[p * each : (p + 1) * each].astype(target.dtype)
        else:
            full[:, : value.shape[1]] = value
            for p in range(count):
                target[p] = full[pl.ds(p * each, each), : value.shape[1]].astype(target.dtype)

    def renorm(k, d):
        vmatrix = jnp.dot(
            left[k, :, d * row_count : (d + 1) * row_count], near_basis[d],
            preferred_element_type=jnp.float32,
        ).astype(jnp.bfloat16)
        value = jnp.dot(basis_t[...], vmatrix, preferred_element_type=jnp.float32)
        cut(stage.at[k * 3 + d], value, op_n, share)

        def send(step, carry):
            peer = lax.rem(op + 1 + lax.rem(step - 1 + op, op_n - 1), op_n)
            piece(k, d, op, peer, peer).start()
            return carry

        lax.fori_loop(1, op_n, send, 0)
        renorm_ref[op * ops + k, :, d * kept : (d + 1) * kept] = stage[k * 3 + d, op]

    for k in range(ops):
        loads[1 + k].wait()
        renorm(k, 1)
        if k == 0:
            halos(near_basis, 0)
    halos(near_psi, 1)

    def side(d):
        @pl.when(has[d])
        def _():
            arrival(near_basis, 0, d).wait_recv()
            for k in range(ops):
                renorm(k, d)

        @pl.when(jnp.logical_not(has[d]))
        def _():
            def clear(g, carry):
                renorm_ref[g, :, d * kept : (d + 1) * kept] = jnp.zeros((share, kept), jnp.bfloat16)
                return carry

            lax.fori_loop(0, op_n * ops, clear, 0)

    side(0)
    side(2)
    loads[2 + ops].wait()

    def sigma_term(k, d):
        product = jnp.dot(
            left[k, :, d * row_count : (d + 1) * row_count], near_psi[d],
            preferred_element_type=jnp.float32,
        ).astype(jnp.bfloat16)
        return lax.dot_general(
            product, right[k, d], (((1,), (1,)), ((), ())), preferred_element_type=jnp.float32
        )

    total[...] = sum(sigma_term(k, 1) for k in range(ops))
    for d in (0, 2):
        @pl.when(has[d])
        def _():
            arrival(near_psi, 1, d).wait_recv()
            total[...] += sum(sigma_term(k, d) for k in range(ops))

    cut(sums, jnp.where(live_state, total[...], 0.0), op_n, sigma_share)

    levels = op_n.bit_length() - 1

    def partner(level):
        return op + (1 - 2 * (op // 2**level % 2)) * 2**level

    def sigma_piece(level, j, mine):
        low = op % 2**level
        here, there = op // 2**level % 2, partner(level) // 2**level % 2
        owner = low + (here if mine else there) * 2**level + j * 2 ** (level + 1)
        slot = op_n - op_n // 2**level + j
        if level == levels - 1:
            source, target = last.at[0], last.at[1]
        else:
            source, target = sums.at[owner], arrived.at[slot]
        return owner, pltpu.make_async_remote_copy(
            src_ref=source, dst_ref=target,
            send_sem=sigma_send.at[slot], recv_sem=sigma_recv.at[slot],
            device_id=(sec, partner(level)), device_id_type=MESH,
        )

    def sigma_start(level):
        for j in range(op_n // 2 ** (level + 1)):
            owner, copy = sigma_piece(level, j, False)
            if level == levels - 1:
                last[0] = sums[owner].astype(jnp.bfloat16)
            copy.start()

    def sigma_add(level):
        for j in range(op_n // 2 ** (level + 1)):
            owner, copy = sigma_piece(level, j, True)
            copy.wait_recv()
            slot = op_n - op_n // 2**level + j
            if level == levels - 1:
                sigma_ref[...] = (sums[owner] + last[1].astype(jnp.float32)).astype(jnp.bfloat16)
            else:
                sums[owner] += arrived[slot]

    sigma_start(0)
    sigma_add(0)
    sigma_start(1)
    for level in range(1, levels):
        sigma_add(level)
        if level + 1 < levels:
            sigma_start(level + 1)

    def finish(k, d):
        def one(step, carry):
            source = lax.rem(op + op_n - step, op_n)
            piece(k, d, source, source, source).wait()
            return carry

        lax.fori_loop(1, op_n, one, 0)

    for k in range(ops):
        finish(k, 1)
    for d in (0, 2):
        @pl.when(has[d])
        def _():
            halo(near_basis, 0, d).wait_send()
            halo(near_psi, 1, d).wait_send()
            for k in range(ops):
                finish(k, d)

    for level in range(levels):
        for j in range(op_n // 2 ** (level + 1)):
            sigma_piece(level, j, False)[1].wait_send()


def deliver(sigma_in, renorm_in, sigma_out, renorm_out, sem):
    copies = (
        pltpu.make_async_copy(sigma_in, sigma_out, sem.at[0]),
        pltpu.make_async_copy(renorm_in, renorm_out, sem.at[1]),
    )
    for copy in copies:
        copy.start()
    for copy in copies:
        copy.wait()


def local(sec_n, op_n, psi_blocks, sector_rows, kept_cols, basis, left_ops, right_ops):
    row_count, width = psi_blocks.shape
    kept = basis.shape[1]
    ops = left_ops.shape[0]
    share = kept // op_n
    sigma_share = row_count // op_n
    bf16 = jnp.bfloat16
    vmem = pl.BlockSpec(memory_space=pltpu.VMEM)
    smem = pl.BlockSpec(memory_space=pltpu.SMEM)
    hbm = pl.BlockSpec(memory_space=pl.ANY)
    dma = pltpu.SemaphoreType.DMA
    results = (
        jax.ShapeDtypeStruct((sigma_share, width), bf16),
        jax.ShapeDtypeStruct((ops * op_n, share, 3 * kept), bf16),
    )
    made = pl.pallas_call(
        functools.partial(kernel, sec_n, op_n),
        out_shape=tuple(pltpu.VMEM(x.shape, x.dtype) for x in results),
        in_specs=[smem, smem, hbm, hbm, hbm, hbm],
        out_specs=(vmem, vmem),
        scratch_shapes=[
            pltpu.VMEM((row_count, width), bf16),
            pltpu.VMEM((row_count, kept), bf16),
            pltpu.VMEM((3, row_count, width), bf16),
            pltpu.VMEM((3, row_count, kept), bf16),
            pltpu.VMEM((kept, row_count), bf16),
            pltpu.VMEM((ops, row_count, 3 * row_count), bf16),
            pltpu.VMEM((ops, 3, width, width), bf16),
            pltpu.VMEM((max(row_count, kept), max(width, kept)), jnp.float32),
            pltpu.VMEM((ops * 3, op_n, share, kept), bf16),
            pltpu.VMEM((row_count, width), jnp.float32),
            pltpu.VMEM((op_n, sigma_share, width), jnp.float32),
            pltpu.VMEM((op_n, sigma_share, width), jnp.float32),
            pltpu.VMEM((2, sigma_share, width), bf16),
            dma((ops + 3,)),
            dma((2, 3)),
            dma((2, 3)),
            dma((ops * 3, op_n)),
            dma((ops * 3, op_n)),
            dma((op_n,)),
            dma((op_n,)),
        ],
        compiler_params=pltpu.CompilerParams(
            collective_id=0, has_side_effects=True, vmem_limit_bytes=56 * 1024 * 1024
        ),
    )(sector_rows, kept_cols, psi_blocks, basis, left_ops, right_ops[:, 0])
    return pl.pallas_call(
        deliver,
        out_shape=results,
        in_specs=[hbm, hbm],
        out_specs=(hbm, hbm),
        scratch_shapes=[dma((2,))],
        compiler_params=pltpu.CompilerParams(vmem_limit_bytes=1024 * 1024),
    )(*made)


def solution(mesh):
    placed = (
        P("sec", None),
        P("sec"),
        P("sec"),
        P("sec", None),
        P("op", "sec", None),
        P("op", "sec", None, None, None),
    )
    return jax.shard_map(
        functools.partial(local, mesh.shape["sec"], mesh.shape["op"]),
        mesh=mesh,
        in_specs=placed,
        out_specs=(P(("sec", "op"), None), P(None, ("sec", "op"), None)),
        check_vma=False,
    )
```
